32 devices in a mesh: pair: 16 (over z, y, core), irrep: 2 (over x).
Axes of the slice: x: 2, y: 2, z: 4, core: 2. Of those that a mesh axis runs over, the one named last changes fastest.
Arguments:
- blocks: bfloat16 [16, 2, 1280, 1280], P(None, 'irrep', 'pair'), may hold values from -6 to 6
- coefficients: bfloat16 [1280, 2048], P(None, 'irrep'), may hold values from -0.15625 to 0.15625
- shell_batch_functions: int32 [1280], replicated, may hold values from 0 to 1279, each once
- irrep_counts: int32 [8], replicated, may hold values from 128 to 256, as said below
- pair_symmetry: int32 [16, 2], P('pair', 'irrep'), may hold values from 0 to 7
Outputs:
- orbital_pair_integrals: float32 [16, 2, 8, 256, 256], P('pair', 'irrep')
The draws below stay inside these ranges and needn't reach their ends.
Inputs may be any that keep to these rules, and one draw needn't show every extreme that they name: `shell_batch_functions`: each AO function appears exactly once. `irrep_counts`: irrep 0 holds all 256 virtual orbitals.
All inputs are finite; a program needn't handle non-finite values.
Results may differ from the reference program's by a relative error of at most 0.0029.
Values may be sent and summed in bfloat16 or wider, within the bound.
A program may use at most 128 MiB of HBM per device.

```python
import jax
import jax.numpy as jnp
from jax import lax

NAO = 1280
VIR = 256
NIRR = 8
PAIRS_A = 16
PAIRS_B = 2


def draw_irrep_counts(key, part):
    remaining_parts = jax.random.randint(key, (NIRR,), VIR // 2, VIR + 1)
    first = jnp.arange(NIRR) == 0
    return jnp.where(first, VIR, remaining_parts).astype(jnp.int32)


def with_ends(drawn, own_key, low, largest):
    extent = drawn.shape
    spot = [jax.random.randint(jax.random.fold_in(own_key, axis), (), 0, extent[axis]) for axis in range(len(extent))]
    drawn = drawn.at[tuple(spot)].set(low)
    longest = extent.index(max(extent))
    spot[longest] = (spot[longest] + 1) % extent[longest]
    return drawn.at[tuple(spot)].set(largest)


def levels(key, extent, cuts, least, largest):
    loudness = 1.0
    for position, parts in cuts:
        heights = jax.random.uniform(jax.random.fold_in(jax.random.fold_in(key, 6), position), (parts,), jnp.float32, least / len(cuts), largest / len(cuts))
        loudness = loudness * jnp.repeat(jnp.exp(heights), extent[position] // parts).reshape((-1,) + (1,) * (len(extent) - 1 - position))
    return loudness


def bell_draw(key, dims, spread, reach, pieces=(), kind=jnp.bfloat16):
    gain = levels(key, dims, pieces, -0.22, 0.18) if pieces else 1.0
    values = jax.random.normal(key, dims, jnp.float32) * spread * gain
    return jnp.minimum(jnp.maximum(values, -reach), reach).astype(kind)


def setup_inputs(seed: int = 0) -> dict:
    keys = jax.random.split(jax.random.key(seed), 6)
    return {
        "blocks": bell_draw(keys[0], (PAIRS_A, PAIRS_B, NAO, NAO), 1.0, 6.0, ((1, 2), (2, 16))),
        "coefficients": bell_draw(keys[1], (NAO, NIRR * VIR), NAO ** -0.5, 0.15625, ((1, 2),)),
        "shell_batch_functions": jax.random.permutation(keys[2], NAO).astype(jnp.int32),
        "irrep_counts": draw_irrep_counts(jax.random.fold_in(keys[5], 71), 0),
        "pair_symmetry": with_ends(jax.random.randint(keys[4], (PAIRS_A, PAIRS_B), 0, 8), jax.random.fold_in(keys[4], 1), 0, 7).astype(jnp.int32),
    }


def reference(blocks, coefficients, shell_batch_functions, irrep_counts, pair_symmetry):
    col = jnp.arange(NIRR * VIR, dtype=jnp.int32)
    owner = col // VIR
    limit = jnp.sum(jnp.where(owner[:, None] == jnp.arange(NIRR, dtype=jnp.int32)[None, :], irrep_counts[None, :], 0), axis=1)
    live = (col % VIR) < limit
    masked = jnp.where(live[None, :], coefficients, jnp.zeros_like(coefficients))
    rows = jnp.take(masked, shell_batch_functions.astype(jnp.int32), axis=0)
    third_row_group = rows.astype(jnp.float32).reshape(NAO, NIRR, VIR)
    flat_blocks = blocks.reshape(PAIRS_A * PAIRS_B, NAO, NAO)
    flat_sym = pair_symmetry.reshape(PAIRS_A * PAIRS_B).astype(jnp.int32)

    def one_pair(args):
        block, symmetry = args
        half = jnp.dot(block, masked, preferred_element_type=jnp.float32).astype(jnp.bfloat16)
        half_three = half.astype(jnp.float32).reshape(NAO, NIRR, VIR)
        partner_irrep = jnp.bitwise_xor(jnp.arange(NIRR, dtype=jnp.int32), symmetry)
        selected_option = jnp.take(half_three, partner_irrep, axis=1)
        return jnp.einsum("ytq,ytj->tqj", third_row_group, selected_option, precision=lax.Precision.HIGHEST)

    result = lax.map(one_pair, (flat_blocks, flat_sym))
    return result.reshape(PAIRS_A, PAIRS_B, NIRR, VIR, VIR)
```

```python
import functools

import jax
import jax.numpy as jnp
from jax import lax
from jax.experimental import pallas as pl
from jax.experimental.pallas import tpu as pltpu
from jax.sharding import PartitionSpec as P

VIR = 256
INNER = 4
MESH = pl.DeviceIdType.MESH


def kernel(
    n, ni, blocks, coef, batch, sym, out,
    recv, c_all, perm, rows_t, half,
    b_send, b_recv, c_send, c_recv, f_send, f_recv, own_sem, c_own_sem,
):
    me = lax.axis_index("pair")
    qi = lax.axis_index("irrep")
    rows = blocks.shape[2]
    nao = coef.shape[0]
    per = coef.shape[1] // VIR
    irr = ni * per
    levels = n // INNER
    h = levels // 2
    lev, inner, core = me // INNER, me % INNER, me % 2
    sibling = me + 1 - 2 * core
    span = INNER * rows

    def level_at(step):
        if step < h:
            return (lev // h) * h + (lev % h + step) % h
        return ((lev // h + 1) % 2) * h + (lev % h + step) % h

    barrier = pltpu.get_barrier_semaphore()
    for k in range(1, n):
        pl.semaphore_signal(barrier, inc=1, device_id=((me + k) % n, qi), device_id_type=MESH)
    for d in range(1, ni):
        pl.semaphore_signal(barrier, inc=1, device_id=(me, (qi + d) % ni), device_id_type=MESH)
    own = pltpu.make_async_copy(blocks.at[me, 0], recv.at[me], own_sem)
    own.start()
    c_own = []
    for j in range(per):
        cp = pltpu.make_async_copy(
            coef.at[:, pl.ds(j * VIR, VIR)], c_all.at[qi * per + j], c_own_sem.at[j]
        )
        cp.start()
        c_own.append(cp)
    pl.semaphore_wait(barrier, n - 1 + ni - 1)

    part = pl.ds(pl.multiple_of(core * (nao // 2), nao // 2), nao // 2)
    other = pl.ds(pl.multiple_of((1 - core) * (nao // 2), nao // 2), nao // 2)
    c_copies = []
    for d in range(1, ni):
        for j in range(per):
            t = (d - 1) * per + j
            cp = pltpu.make_async_remote_copy(
                src_ref=coef.at[part, pl.ds(j * VIR, VIR)],
                dst_ref=c_all.at[qi * per + j, part],
                send_sem=c_send.at[t],
                recv_sem=c_recv.at[t],
                device_id=(me, (qi + d) % ni),
                device_id_type=MESH,
            )
            cp.start()
            c_copies.append(cp)

    b_copies = []
    for step in list(range(h, levels)) + list(range(h - 1, -1, -1)):
        for i in range(INNER):
            if step == 0 and i == 0:
                continue
            to = level_at(step) * INNER + (inner + i) % INNER
            cp = pltpu.make_async_remote_copy(
                src_ref=blocks.at[to, 0],
                dst_ref=recv.at[me],
                send_sem=b_send.at[to],
                recv_sem=b_recv.at[me],
                device_id=(to, qi),
                device_id_type=MESH,
            )
            cp.start()
            b_copies.append(cp)

    strip = 128

    @pl.loop(0, nao // strip)
    def _(k):
        base = pl.multiple_of(k * strip, strip)
        nu = lax.broadcasted_iota(jnp.int32, (strip, nao), 0) + base
        perm[pl.ds(base, strip), :] = jnp.where(nu == batch[...], 1.0, 0.0).astype(jnp.bfloat16)

    f_copies = []
    for d in range(1, ni):
        for j in range(per):
            t = (d - 1) * per + j
            slab = ((qi + ni - d) % ni) * per + j
            c_copies[t].wait_recv()
            cp = pltpu.make_async_remote_copy(
                src_ref=c_all.at[slab, part],
                dst_ref=c_all.at[slab, part],
                send_sem=f_send.at[t],
                recv_sem=f_recv.at[t],
                device_id=(sibling, qi),
                device_id_type=MESH,
            )
            cp.start()
            f_copies.append((cp, slab, t))
    for cp in c_own:
        cp.wait()
    for cp, slab, t in f_copies:
        cp.wait_recv()

    @pl.loop(0, irr)
    def _(r):
        rows_t[r] = lax.dot_general(
            c_all[r], perm[...], (((0,), (0,)), ((), ())), preferred_element_type=jnp.float32
        ).astype(jnp.bfloat16)

    own.wait()
    for step in range(levels):
        lv = level_at(step)
        for i in range(INNER):
            if step == 0 and i == 0:
                continue
            src = lv * INNER + (inner + i) % INNER
            pltpu.make_async_remote_copy(
                src_ref=blocks.at[src, 0],
                dst_ref=recv.at[src],
                send_sem=b_send.at[src],
                recv_sem=b_recv.at[src],
                device_id=(src, qi),
                device_id_type=MESH,
            ).wait_recv()
        base = pl.multiple_of(lv * span, span)

        @pl.loop(0, irr)
        def _(c):
            x = recv[pl.ds(lv * INNER, INNER)].reshape(span, nao)
            half[c, pl.ds(base, span), :] = jnp.dot(
                x, c_all[c], preferred_element_type=jnp.float32
            ).astype(jnp.bfloat16)

    s = sym[0, 0]

    @pl.loop(0, irr)
    def _(r):
        out[r] = jnp.dot(
            rows_t[r], half[jnp.bitwise_xor(r, s)], preferred_element_type=jnp.float32
        )

    for cp in c_copies + b_copies:
        cp.wait_send()
    for cp, _, _ in f_copies:
        cp.wait_send()


def body(n, ni, blocks, coefficients, shell_batch_functions, irrep_counts, pair_symmetry):
    rows, nao = blocks.shape[2], blocks.shape[3]
    per = coefficients.shape[1] // VIR
    irr = per * ni
    remote = max(1, (ni - 1) * per)
    dma = pltpu.SemaphoreType.DMA
    full = pl.pallas_call(
        functools.partial(kernel, n, ni),
        out_shape=jax.ShapeDtypeStruct((irr, VIR, VIR), jnp.float32),
        in_specs=[
            pl.BlockSpec(memory_space=pl.ANY),
            pl.BlockSpec(memory_space=pl.ANY),
            pl.BlockSpec(memory_space=pltpu.VMEM),
            pl.BlockSpec(memory_space=pltpu.SMEM),
        ],
        out_specs=pl.BlockSpec(memory_space=pltpu.VMEM),
        scratch_shapes=[
            pltpu.VMEM((n, rows, nao), jnp.bfloat16),
            pltpu.VMEM((irr, nao, VIR), jnp.bfloat16),
            pltpu.VMEM((nao, nao), jnp.bfloat16),
            pltpu.VMEM((irr, VIR, nao), jnp.bfloat16),
            pltpu.VMEM((irr, nao, VIR), jnp.bfloat16),
            dma((n,)), dma((n,)), dma((remote,)), dma((remote,)),
            dma((remote,)), dma((remote,)), dma, dma((per,)),
        ],
        compiler_params=pltpu.CompilerParams(
            collective_id=0, has_side_effects=True, vmem_limit_bytes=56 * 2**20
        ),
    )(blocks, coefficients, shell_batch_functions.reshape(1, nao), pair_symmetry)
    label = jnp.arange(irr, dtype=jnp.int32)
    left = irrep_counts
    right = jnp.take(irrep_counts, jnp.bitwise_xor(label, pair_symmetry[0, 0]))
    col = jnp.arange(VIR, dtype=jnp.int32)
    live = (col[None, :, None] < left[:, None, None]) & (col[None, None, :] < right[:, None, None])
    return jnp.where(live, full, 0.0)[None, None]


def solution(mesh):
    in_specs = (P(None, "irrep", "pair", None), P(None, "irrep"), P(), P(), P("pair", "irrep"))
    out_specs = P("pair", "irrep", None, None, None)
    return jax.shard_map(
        functools.partial(body, mesh.shape["pair"], mesh.shape["irrep"]),
        mesh=mesh, in_specs=in_specs, out_specs=out_specs, check_vma=False,
    )
```

```python
import functools

import jax
import jax.numpy as jnp
from jax import lax
from jax.experimental import pallas as pl
from jax.experimental.pallas import tpu as pltpu
from jax.sharding import PartitionSpec as P

VIR = 256
INNER = 4
MESH = pl.DeviceIdType.MESH


def kernel(
    n, ni, blocks, coef, batch, sym, sym_v, out,
    recv, c_all, perm, rows_t, half,
    b_send, b_recv, c_send, c_recv, f_send, f_recv, own_sem, c_own_sem,
    rel_rows, rel_half, p_out, p_in, sym_in, sym_s,
    a_send, a_recv, p_send, p_recv, s_send, s_recv, a_own_sem, s_own_sem,
):
    me = lax.axis_index("pair")
    qi = lax.axis_index("irrep")
    rows = blocks.shape[2]
    nao = coef.shape[0]
    per = coef.shape[1] // VIR
    irr = ni * per
    levels = n // INNER
    h = levels // 2
    lev, inner, core = me // INNER, me % INNER, me % 2
    sibling = me + 1 - 2 * core
    span = INNER * rows
    relay = levels == 4
    hf = lev // h
    half_rows = h * span
    half_base = pl.multiple_of(hf * half_rows, half_rows)
    is_mid = ((lev + 1) // 2) % 2 == 1
    is_end = ((lev + 1) // 2) % 2 == 0
    own_mid, far_mid, far_end = 1 + hf, 2 - hf, 3 * (1 - hf)

    def level_at(step):
        if step < h:
            return (lev // h) * h + (lev % h + step) % h
        return ((lev // h + 1) % 2) * h + (lev % h + step) % h

    barrier = pltpu.get_barrier_semaphore()
    for k in range(1, n):
        pl.semaphore_signal(barrier, inc=1, device_id=((me + k) % n, qi), device_id_type=MESH)
    for d in range(1, ni):
        pl.semaphore_signal(barrier, inc=1, device_id=(me, (qi + d) % ni), device_id_type=MESH)
    own = pltpu.make_async_copy(blocks.at[me, 0], recv.at[me], own_sem)
    own.start()
    c_own = []
    for j in range(per):
        cp = pltpu.make_async_copy(
            coef.at[:, pl.ds(j * VIR, VIR)], c_all.at[qi * per + j], c_own_sem.at[j]
        )
        cp.start()
        c_own.append(cp)
    pl.semaphore_wait(barrier, n - 1 + ni - 1)

    part = pl.ds(pl.multiple_of(core * (nao // 2), nao // 2), nao // 2)
    other = pl.ds(pl.multiple_of((1 - core) * (nao // 2), nao // 2), nao // 2)
    c_copies = []
    for d in range(1, ni):
        for j in range(per):
            t = (d - 1) * per + j
            cp = pltpu.make_async_remote_copy(
                src_ref=coef.at[part, pl.ds(j * VIR, VIR)],
                dst_ref=c_all.at[qi * per + j, part],
                send_sem=c_send.at[t],
                recv_sem=c_recv.at[t],
                device_id=(me, (qi + d) % ni),
                device_id_type=MESH,
            )
            cp.start()
            c_copies.append(cp)

    def relay_copy(i, at):
        to = own_mid * INNER + i
        return pltpu.make_async_remote_copy(
            src_ref=blocks.at[far_end * INNER + i, 0],
            dst_ref=rel_rows.at[at],
            send_sem=a_send.at[i],
            recv_sem=a_recv.at[at],
            device_id=(to, qi),
            device_id_type=MESH,
        )

    my_slot = me - hf * h * INNER
    a_local = pltpu.make_async_copy(
        blocks.at[far_end * INNER + inner, 0], rel_rows.at[my_slot], a_own_sem
    )
    s_copy = pltpu.make_async_remote_copy(
        src_ref=sym_v, dst_ref=sym_in, send_sem=s_send, recv_sem=s_recv,
        device_id=(far_mid * INNER + inner, qi), device_id_type=MESH,
    )
    if relay:
        for k in range(1, INNER):
            relay_copy((inner + k) % INNER, my_slot).start()

        @pl.when(is_mid)
        def _():
            a_local.start()

        @pl.when(is_end)
        def _():
            s_copy.start()
            relay_copy(inner, my_slot).start()

        order = [None] + list(range(h - 1, -1, -1))
    else:
        order = list(range(h, levels)) + list(range(h - 1, -1, -1))

    b_copies = []
    for step in order:
        for i in range(INNER):
            if step == 0 and i == 0:
                continue
            target = far_mid if step is None else level_at(step)
            to = target * INNER + (inner + i) % INNER
            cp = pltpu.make_async_remote_copy(
                src_ref=blocks.at[to, 0],
                dst_ref=recv.at[me],
                send_sem=b_send.at[to],
                recv_sem=b_recv.at[me],
                device_id=(to, qi),
                device_id_type=MESH,
            )
            cp.start()
            b_copies.append(cp)

    strip = 128

    @pl.loop(0, nao // strip)
    def _(k):
        base = pl.multiple_of(k * strip, strip)
        nu = lax.broadcasted_iota(jnp.int32, (strip, nao), 0) + base
        perm[pl.ds(base, strip), :] = jnp.where(nu == batch[...], 1.0, 0.0).astype(jnp.bfloat16)

    def make_rows_t(r):
        rows_t[r] = lax.dot_general(
            c_all[r], perm[...], (((0,), (0,)), ((), ())), preferred_element_type=jnp.float32
        ).astype(jnp.bfloat16)

    for cp in c_own:
        cp.wait()

    @pl.loop(0, per)
    def _(j):
        make_rows_t(qi * per + j)

    f_copies = []
    for d in range(1, ni):
        for j in range(per):
            t = (d - 1) * per + j
            slab = ((qi + ni - d) % ni) * per + j
            c_copies[t].wait_recv()
            cp = pltpu.make_async_remote_copy(
                src_ref=c_all.at[slab, part],
                dst_ref=c_all.at[slab, part],
                send_sem=f_send.at[t],
                recv_sem=f_recv.at[t],
                device_id=(sibling, qi),
                device_id_type=MESH,
            )
            cp.start()
            f_copies.append((cp, slab, t))
            if t >= 1:
                prev, prev_slab, _ = f_copies[t - 1]
                prev.wait_recv()
                make_rows_t(prev_slab)
    last, last_slab, _ = f_copies[-1]
    last.wait_recv()
    make_rows_t(last_slab)

    def p_copy(r):
        return pltpu.make_async_remote_copy(
            src_ref=p_out.at[r], dst_ref=p_in.at[r],
            send_sem=p_send.at[r], recv_sem=p_recv.at[r],
            device_id=(far_end * INNER + inner, qi), device_id_type=MESH,
        )

    if relay:

        @pl.when(is_mid)
        def _():
            s_copy.wait_recv()
            to_smem = pltpu.make_async_copy(sym_in, sym_s, s_own_sem)
            to_smem.start()
            a_local.wait()
            for step in range(h):
                for i in range(INNER):
                    if step == 0 and i == 0:
                        continue
                    at = ((lev % h + step) % h) * INNER + (inner + i) % INNER
                    relay_copy(inner, at).wait_recv()
            to_smem.wait()

            @pl.loop(0, irr)
            def _(c):
                x = rel_rows[...].reshape(half_rows, nao)
                rel_half[c] = jnp.dot(
                    x, c_all[c], preferred_element_type=jnp.float32
                ).astype(jnp.bfloat16)

            their = sym_s[0, 0]

            @pl.loop(0, irr)
            def _(r):
                p_out[r] = jnp.dot(
                    rows_t[r, :, pl.ds(half_base, half_rows)],
                    rel_half[jnp.bitwise_xor(r, their)],
                    preferred_element_type=jnp.float32,
                ).astype(jnp.bfloat16)
                p_copy(r).start()

    own.wait()

    def do_level(step):
        lv = level_at(step)
        for i in range(INNER):
            if step == 0 and i == 0:
                continue
            src = lv * INNER + (inner + i) % INNER
            pltpu.make_async_remote_copy(
                src_ref=blocks.at[src, 0],
                dst_ref=recv.at[src],
                send_sem=b_send.at[src],
                recv_sem=b_recv.at[src],
                device_id=(src, qi),
                device_id_type=MESH,
            ).wait_recv()
        base = pl.multiple_of(lv * span, span)

        @pl.loop(0, irr)
        def _(c):
            x = recv[pl.ds(lv * INNER, INNER)].reshape(span, nao)
            half[c, pl.ds(base, span), :] = jnp.dot(
                x, c_all[c], preferred_element_type=jnp.float32
            ).astype(jnp.bfloat16)

    s = sym[0, 0]

    def finish_all():
        @pl.loop(0, irr)
        def _(r):
            out[r] = jnp.dot(
                rows_t[r], half[jnp.bitwise_xor(r, s)], preferred_element_type=jnp.float32
            )

    if relay:
        for step in range(h):
            do_level(step)

        @pl.when(is_mid)
        def _():
            for step in range(h, levels):
                do_level(step)
            finish_all()
            for k in range(1, INNER):
                relay_copy((inner + k) % INNER, my_slot).wait_send()

            @pl.loop(0, irr)
            def _(r):
                p_copy(r).wait_send()

        @pl.when(is_end)
        def _():
            @pl.loop(0, irr)
            def _(r):
                out[r] = jnp.dot(
                    rows_t[r, :, pl.ds(half_base, half_rows)],
                    half[jnp.bitwise_xor(r, s), pl.ds(half_base, half_rows), :],
                    preferred_element_type=jnp.float32,
                )

            @pl.loop(0, irr)
            def _(r):
                p_copy(r).wait_recv()
                out[r] = out[r] + p_in[r].astype(jnp.float32)

            for k in range(INNER):
                relay_copy((inner + k) % INNER, my_slot).wait_send()
            s_copy.wait_send()
    else:
        for step in range(levels):
            do_level(step)
        finish_all()

    for cp in c_copies + b_copies:
        cp.wait_send()
    for cp, _, _ in f_copies:
        cp.wait_send()


def body(n, ni, blocks, coefficients, shell_batch_functions, irrep_counts, pair_symmetry):
    rows, nao = blocks.shape[2], blocks.shape[3]
    per = coefficients.shape[1] // VIR
    irr = per * ni
    remote = max(1, (ni - 1) * per)
    dma = pltpu.SemaphoreType.DMA
    full = pl.pallas_call(
        functools.partial(kernel, n, ni),
        out_shape=jax.ShapeDtypeStruct((irr, VIR, VIR), jnp.float32),
        in_specs=[
            pl.BlockSpec(memory_space=pl.ANY),
            pl.BlockSpec(memory_space=pl.ANY),
            pl.BlockSpec(memory_space=pltpu.VMEM),
            pl.BlockSpec(memory_space=pltpu.SMEM),
            pl.BlockSpec(memory_space=pltpu.VMEM),
        ],
        out_specs=pl.BlockSpec(memory_space=pltpu.VMEM),
        scratch_shapes=[
            pltpu.VMEM((n, rows, nao), jnp.bfloat16),
            pltpu.VMEM((irr, nao, VIR), jnp.bfloat16),
            pltpu.VMEM((nao, nao), jnp.bfloat16),
            pltpu.VMEM((irr, VIR, nao), jnp.bfloat16),
            pltpu.VMEM((irr, nao, VIR), jnp.bfloat16),
            dma((n,)), dma((n,)), dma((remote,)), dma((remote,)),
            dma((remote,)), dma((remote,)), dma, dma((per,)),
            pltpu.VMEM((n // 2, rows, nao), jnp.bfloat16),
            pltpu.VMEM((irr, nao // 2, VIR), jnp.bfloat16),
            pltpu.VMEM((irr, VIR, VIR), jnp.bfloat16),
            pltpu.VMEM((irr, VIR, VIR), jnp.bfloat16),
            pltpu.VMEM((8, 128), jnp.int32),
            pltpu.SMEM((8, 128), jnp.int32),
            dma((INNER,)), dma((n // 2,)), dma((irr,)), dma((irr,)),
            dma, dma, dma, dma,
        ],
        compiler_params=pltpu.CompilerParams(
            collective_id=0, has_side_effects=True, vmem_limit_bytes=56 * 2**20
        ),
    )(blocks, coefficients, shell_batch_functions.reshape(1, nao), pair_symmetry,
      jnp.broadcast_to(pair_symmetry, (8, 128)))
    label = jnp.arange(irr, dtype=jnp.int32)
    left = irrep_counts
    right = jnp.take(irrep_counts, jnp.bitwise_xor(label, pair_symmetry[0, 0]))
    col = jnp.arange(VIR, dtype=jnp.int32)
    live = (col[None, :, None] < left[:, None, None]) & (col[None, None, :] < right[:, None, None])
    return jnp.where(live, full, 0.0)[None, None]


def solution(mesh):
    in_specs = (P(None, "irrep", "pair", None), P(None, "irrep"), P(), P(), P("pair", "irrep"))
    out_specs = P("pair", "irrep", None, None, None)
    return jax.shard_map(
        functools.partial(body, mesh.shape["pair"], mesh.shape["irrep"]),
        mesh=mesh, in_specs=in_specs, out_specs=out_specs, check_vma=False,
    )
```

```python
import functools

import jax
import jax.numpy as jnp
from jax import lax
from jax.experimental import pallas as pl
from jax.experimental.pallas import tpu as pltpu
from jax.sharding import PartitionSpec as P

VIR = 256
INNER = 4
MESH = pl.DeviceIdType.MESH


def kernel(
    n, ni, blocks, coef, batch, sym, out,
    recv, c_all, perm, rows_t, half,
    b_send, b_recv, c_send, c_recv, f_send, f_recv, own_sem, c_own_sem,
    rel_rows, rel_half, p_out, p_in, sym_v, sym_in, sym_s,
    a_send, a_recv, p_send, p_recv, s_send, s_recv, a_own_sem, s_own_sem,
):
    me = lax.axis_index("pair")
    qi = lax.axis_index("irrep")
    rows = blocks.shape[2]
    nao = coef.shape[0]
    per = coef.shape[1] // VIR
    irr = ni * per
    levels = n // INNER
    h = levels // 2
    lev, inner, core = me // INNER, me % INNER, me % 2
    sibling = me + 1 - 2 * core
    span = INNER * rows
    relay = levels == 4
    hf = lev // h
    half_rows = h * span
    half_base = pl.multiple_of(hf * half_rows, half_rows)
    is_mid = ((lev + 1) // 2) % 2 == 1
    is_end = ((lev + 1) // 2) % 2 == 0
    own_mid, far_mid, far_end = 1 + hf, 2 - hf, 3 * (1 - hf)

    def level_at(step):
        if step < h:
            return (lev // h) * h + (lev % h + step) % h
        return ((lev // h + 1) % 2) * h + (lev % h + step) % h

    barrier = pltpu.get_barrier_semaphore()
    for k in range(1, n):
        pl.semaphore_signal(barrier, inc=1, device_id=((me + k) % n, qi), device_id_type=MESH)
    for d in range(1, ni):
        pl.semaphore_signal(barrier, inc=1, device_id=(me, (qi + d) % ni), device_id_type=MESH)
    own = pltpu.make_async_copy(blocks.at[me, 0], recv.at[me], own_sem)
    own.start()
    c_own = []
    for j in range(per):
        cp = pltpu.make_async_copy(
            coef.at[:, pl.ds(j * VIR, VIR)], c_all.at[qi * per + j], c_own_sem.at[j]
        )
        cp.start()
        c_own.append(cp)
    pl.semaphore_wait(barrier, n - 1 + ni - 1)

    part = pl.ds(pl.multiple_of(core * (nao // 2), nao // 2), nao // 2)
    other = pl.ds(pl.multiple_of((1 - core) * (nao // 2), nao // 2), nao // 2)
    c_copies = []
    for d in range(1, ni):
        for j in range(per):
            t = (d - 1) * per + j
            cp = pltpu.make_async_remote_copy(
                src_ref=coef.at[part, pl.ds(j * VIR, VIR)],
                dst_ref=c_all.at[qi * per + j, part],
                send_sem=c_send.at[t],
                recv_sem=c_recv.at[t],
                device_id=(me, (qi + d) % ni),
                device_id_type=MESH,
            )
            cp.start()
            c_copies.append(cp)

    def relay_copy(i, at):
        to = own_mid * INNER + i
        return pltpu.make_async_remote_copy(
            src_ref=blocks.at[far_end * INNER + i, 0],
            dst_ref=rel_rows.at[at],
            send_sem=a_send.at[i],
            recv_sem=a_recv.at[at],
            device_id=(to, qi),
            device_id_type=MESH,
        )

    my_slot = me - hf * h * INNER
    a_local = pltpu.make_async_copy(
        blocks.at[far_end * INNER + inner, 0], rel_rows.at[my_slot], a_own_sem
    )
    s_copy = pltpu.make_async_remote_copy(
        src_ref=sym_v, dst_ref=sym_in, send_sem=s_send, recv_sem=s_recv,
        device_id=(far_mid * INNER + inner, qi), device_id_type=MESH,
    )
    if relay:
        for k in range(1, INNER):
            relay_copy((inner + k) % INNER, my_slot).start()

        @pl.when(is_mid)
        def _():
            a_local.start()

        @pl.when(is_end)
        def _():
            sym_v[...] = jnp.full((8, 128), sym[0, 0], jnp.int32)
            s_copy.start()
            relay_copy(inner, my_slot).start()

        order = [None] + list(range(h - 1, -1, -1))
    else:
        order = list(range(h, levels)) + list(range(h - 1, -1, -1))

    b_copies = []
    near_copies = []
    for step in order:
        for i in range(INNER):
            if step == 0 and i == 0:
                continue
            target = far_mid if step is None else level_at(step)
            to = target * INNER + (inner + i) % INNER
            cp = pltpu.make_async_remote_copy(
                src_ref=blocks.at[to, 0],
                dst_ref=recv.at[me],
                send_sem=b_send.at[to],
                recv_sem=b_recv.at[me],
                device_id=(to, qi),
                device_id_type=MESH,
            )
            (b_copies if step is None or step >= h else near_copies).append(cp)

    def start(copies):
        for cp in copies:
            cp.start()

    if relay:

        @pl.when(is_mid)
        def _():
            start(b_copies + near_copies)
    else:
        start(b_copies + near_copies)

    strip = 128

    @pl.loop(0, nao // strip)
    def _(k):
        base = pl.multiple_of(k * strip, strip)
        nu = lax.broadcasted_iota(jnp.int32, (strip, nao), 0) + base
        perm[pl.ds(base, strip), :] = jnp.where(nu == batch[...][None, :], 1.0, 0.0).astype(jnp.bfloat16)

    def make_rows_t(r):
        rows_t[r] = lax.dot_general(
            c_all[r], perm[...], (((0,), (0,)), ((), ())), preferred_element_type=jnp.float32
        ).astype(jnp.bfloat16)

    for cp in c_own:
        cp.wait()

    @pl.loop(0, per)
    def _(j):
        make_rows_t(qi * per + j)

    if relay:

        @pl.when(is_end)
        def _():
            start(b_copies)

    def relay_transform(slab):
        x = rel_rows[...].reshape(half_rows, nao)
        rel_half[slab] = jnp.dot(
            x, c_all[slab], preferred_element_type=jnp.float32
        ).astype(jnp.bfloat16)

    early = (ni - 1) * per - 2

    def relay_early():
        a_local.wait()
        for step in range(h):
            for i in range(INNER):
                if step == 0 and i == 0:
                    continue
                at = ((lev % h + step) % h) * INNER + (inner + i) % INNER
                relay_copy(inner, at).wait_recv()

        @pl.loop(0, per)
        def _(j):
            relay_transform(qi * per + j)

    f_copies = []
    for d in range(1, ni):
        for j in range(per):
            t = (d - 1) * per + j
            slab = ((qi + ni - d) % ni) * per + j
            c_copies[t].wait_recv()
            cp = pltpu.make_async_remote_copy(
                src_ref=c_all.at[slab, part],
                dst_ref=c_all.at[slab, part],
                send_sem=f_send.at[t],
                recv_sem=f_recv.at[t],
                device_id=(sibling, qi),
                device_id_type=MESH,
            )
            cp.start()
            f_copies.append((cp, slab, t))
            if t >= 1:
                prev, prev_slab, _ = f_copies[t - 1]
                prev.wait_recv()
                make_rows_t(prev_slab)
            if relay and t == early:
                pl.when(is_mid)(relay_early)
    if relay:

        @pl.when(is_end)
        def _():
            start(near_copies)

    last, last_slab, _ = f_copies[-1]
    last.wait_recv()
    make_rows_t(last_slab)

    def p_copy(r):
        return pltpu.make_async_remote_copy(
            src_ref=p_out.at[r], dst_ref=p_in.at[r],
            send_sem=p_send.at[r], recv_sem=p_recv.at[r],
            device_id=(far_end * INNER + inner, qi), device_id_type=MESH,
        )

    if relay:

        @pl.when(is_mid)
        def _():
            s_copy.wait_recv()
            to_smem = pltpu.make_async_copy(sym_in, sym_s, s_own_sem)
            to_smem.start()
            to_smem.wait()

            @pl.loop(per, irr)
            def _(k):
                relay_transform((qi * per + k) % irr)

            their = sym_s[0, 0]

            @pl.loop(0, irr)
            def _(r):
                p_out[r] = jnp.dot(
                    rows_t[r, :, pl.ds(half_base, half_rows)],
                    rel_half[jnp.bitwise_xor(r, their)],
                    preferred_element_type=jnp.float32,
                ).astype(jnp.bfloat16)
                p_copy(r).start()

    own.wait()

    def do_level(step):
        lv = level_at(step)
        for i in range(INNER):
            if step == 0 and i == 0:
                continue
            src = lv * INNER + (inner + i) % INNER
            pltpu.make_async_remote_copy(
                src_ref=blocks.at[src, 0],
                dst_ref=recv.at[src],
                send_sem=b_send.at[src],
                recv_sem=b_recv.at[src],
                device_id=(src, qi),
                device_id_type=MESH,
            ).wait_recv()
        base = pl.multiple_of(lv * span, span)

        @pl.loop(0, irr)
        def _(c):
            x = recv[pl.ds(lv * INNER, INNER)].reshape(span, nao)
            half[c, pl.ds(base, span), :] = jnp.dot(
                x, c_all[c], preferred_element_type=jnp.float32
            ).astype(jnp.bfloat16)

    s = sym[0, 0]

    def finish_all():
        @pl.loop(0, irr)
        def _(r):
            out[r] = jnp.dot(
                rows_t[r], half[jnp.bitwise_xor(r, s)], preferred_element_type=jnp.float32
            )

    if relay:
        other_base = pl.multiple_of((1 - hf) * half_rows, half_rows)

        def folded(r, base):
            return jnp.dot(
                rows_t[r, :, pl.ds(base, half_rows)],
                half[jnp.bitwise_xor(r, s), pl.ds(base, half_rows), :],
                preferred_element_type=jnp.float32,
            )

        do_level(0)

        @pl.when(is_mid)
        def _():
            for step in range(h, levels):
                do_level(step)

            @pl.loop(0, irr)
            def _(r):
                out[r] = folded(r, other_base)

        do_level(1)

        @pl.when(is_mid)
        def _():
            @pl.loop(0, irr)
            def _(r):
                out[r] = out[r] + folded(r, half_base)

            for k in range(1, INNER):
                relay_copy((inner + k) % INNER, my_slot).wait_send()

            @pl.loop(0, irr)
            def _(r):
                p_copy(r).wait_send()

        @pl.when(is_end)
        def _():
            @pl.loop(0, irr)
            def _(r):
                out[r] = folded(r, half_base)

            @pl.loop(0, irr)
            def _(r):
                p_copy(r).wait_recv()
                out[r] = out[r] + p_in[r].astype(jnp.float32)

            for k in range(INNER):
                relay_copy((inner + k) % INNER, my_slot).wait_send()
            s_copy.wait_send()
    else:
        for step in range(levels):
            do_level(step)
        finish_all()

    for cp in c_copies + b_copies + near_copies:
        cp.wait_send()
    for cp, _, _ in f_copies:
        cp.wait_send()


def body(n, ni, blocks, coefficients, shell_batch_functions, irrep_counts, pair_symmetry):
    rows, nao = blocks.shape[2], blocks.shape[3]
    per = coefficients.shape[1] // VIR
    irr = per * ni
    remote = max(1, (ni - 1) * per)
    dma = pltpu.SemaphoreType.DMA
    full = pl.pallas_call(
        functools.partial(kernel, n, ni),
        out_shape=jax.ShapeDtypeStruct((irr, VIR, VIR), jnp.float32),
        in_specs=[
            pl.BlockSpec(memory_space=pl.ANY),
            pl.BlockSpec(memory_space=pl.ANY),
            pl.BlockSpec(memory_space=pltpu.VMEM),
            pl.BlockSpec(memory_space=pltpu.SMEM),
        ],
        out_specs=pl.BlockSpec(memory_space=pltpu.VMEM),
        scratch_shapes=[
            pltpu.VMEM((n, rows, nao), jnp.bfloat16),
            pltpu.VMEM((irr, nao, VIR), jnp.bfloat16),
            pltpu.VMEM((nao, nao), jnp.bfloat16),
            pltpu.VMEM((irr, VIR, nao), jnp.bfloat16),
            pltpu.VMEM((irr, nao, VIR), jnp.bfloat16),
            dma((n,)), dma((n,)), dma((remote,)), dma((remote,)),
            dma((remote,)), dma((remote,)), dma, dma((per,)),
            pltpu.VMEM((n // 2, rows, nao), jnp.bfloat16),
            pltpu.VMEM((irr, nao // 2, VIR), jnp.bfloat16),
            pltpu.VMEM((irr, VIR, VIR), jnp.bfloat16),
            pltpu.VMEM((irr, VIR, VIR), jnp.bfloat16),
            pltpu.VMEM((8, 128), jnp.int32),
            pltpu.VMEM((8, 128), jnp.int32),
            pltpu.SMEM((8, 128), jnp.int32),
            dma((INNER,)), dma((n // 2,)), dma((irr,)), dma((irr,)),
            dma, dma, dma, dma,
        ],
        compiler_params=pltpu.CompilerParams(
            collective_id=0, has_side_effects=True, vmem_limit_bytes=56 * 2**20
        ),
    )(blocks, coefficients, shell_batch_functions, pair_symmetry)
    label = jnp.arange(irr, dtype=jnp.int32)
    left = irrep_counts
    partner = jnp.bitwise_xor(label, pair_symmetry[0, 0])
    right = jnp.sum(jnp.where(partner[:, None] == label[None, :], irrep_counts[None, :], 0), axis=1)
    col = jnp.arange(VIR, dtype=jnp.int32)
    live = (col[None, :, None] < left[:, None, None]) & (col[None, None, :] < right[:, None, None])
    return jnp.where(live, full, 0.0)[None, None]


def solution(mesh):
    in_specs = (P(None, "irrep", "pair", None), P(None, "irrep"), P(), P(), P("pair", "irrep"))
    out_specs = P("pair", "irrep", None, None, None)
    return jax.shard_map(
        functools.partial(body, mesh.shape["pair"], mesh.shape["irrep"]),
        mesh=mesh, in_specs=in_specs, out_specs=out_specs, check_vma=False,
    )
```

```python
import functools

import jax
import jax.numpy as jnp
from jax import lax
from jax.experimental import pallas as pl
from jax.experimental.pallas import tpu as pltpu
from jax.sharding import PartitionSpec as P

VIR = 256
INNER = 4
MESH = pl.DeviceIdType.MESH


def kernel(
    n, ni, blocks, coef, batch, sym, counts, out,
    recv, c_all, perm, rows_t, half,
    b_send, b_recv, c_send, c_recv, f_send, f_recv, own_sem, c_own_sem,
    rel_rows, rel_half, p_out, p_in, sym_v, sym_in, sym_s,
    a_send, a_recv, p_send, p_recv, s_send, s_recv, a_own_sem, s_own_sem,
):
    me = lax.axis_index("pair")
    qi = lax.axis_index("irrep")
    rows = blocks.shape[2]
    nao = coef.shape[0]
    per = coef.shape[1] // VIR
    irr = ni * per
    levels = n // INNER
    h = levels // 2
    lev, inner, core = me // INNER, me % INNER, me % 2
    sibling = me + 1 - 2 * core
    span = INNER * rows
    relay = levels == 4
    hf = lev // h
    half_rows = h * span
    half_base = pl.multiple_of(hf * half_rows, half_rows)
    is_mid = ((lev + 1) // 2) % 2 == 1
    is_end = ((lev + 1) // 2) % 2 == 0
    own_mid, far_mid, far_end = 1 + hf, 2 - hf, 3 * (1 - hf)

    def level_at(step):
        if step < h:
            return (lev // h) * h + (lev % h + step) % h
        return ((lev // h + 1) % 2) * h + (lev % h + step) % h

    barrier = pltpu.get_barrier_semaphore()
    for k in range(1, n):
        pl.semaphore_signal(barrier, inc=1, device_id=((me + k) % n, qi), device_id_type=MESH)
    for d in range(1, ni):
        pl.semaphore_signal(barrier, inc=1, device_id=(me, (qi + d) % ni), device_id_type=MESH)
    own = pltpu.make_async_copy(blocks.at[me, 0], recv.at[me], own_sem)
    own.start()
    c_own = []
    for j in range(per):
        cp = pltpu.make_async_copy(
            coef.at[:, pl.ds(j * VIR, VIR)], c_all.at[qi * per + j], c_own_sem.at[j]
        )
        cp.start()
        c_own.append(cp)
    pl.semaphore_wait(barrier, n - 1 + ni - 1)

    part = pl.ds(pl.multiple_of(core * (nao // 2), nao // 2), nao // 2)
    other = pl.ds(pl.multiple_of((1 - core) * (nao // 2), nao // 2), nao // 2)
    c_copies = []
    for d in range(1, ni):
        for j in range(per):
            t = (d - 1) * per + j
            cp = pltpu.make_async_remote_copy(
                src_ref=coef.at[part, pl.ds(j * VIR, VIR)],
                dst_ref=c_all.at[qi * per + j, part],
                send_sem=c_send.at[t],
                recv_sem=c_recv.at[t],
                device_id=(me, (qi + d) % ni),
                device_id_type=MESH,
            )
            cp.start()
            c_copies.append(cp)

    def relay_copy(i, at):
        to = own_mid * INNER + i
        return pltpu.make_async_remote_copy(
            src_ref=blocks.at[far_end * INNER + i, 0],
            dst_ref=rel_rows.at[at],
            send_sem=a_send.at[i],
            recv_sem=a_recv.at[at],
            device_id=(to, qi),
            device_id_type=MESH,
        )

    my_slot = me - hf * h * INNER
    a_local = pltpu.make_async_copy(
        blocks.at[far_end * INNER + inner, 0], rel_rows.at[my_slot], a_own_sem
    )
    s_copy = pltpu.make_async_remote_copy(
        src_ref=sym_v, dst_ref=sym_in, send_sem=s_send, recv_sem=s_recv,
        device_id=(far_mid * INNER + inner, qi), device_id_type=MESH,
    )
    if relay:
        for k in range(1, INNER):
            relay_copy((inner + k) % INNER, my_slot).start()

        @pl.when(is_mid)
        def _():
            a_local.start()

        @pl.when(is_end)
        def _():
            sym_v[...] = jnp.full((8, 128), sym[0, 0], jnp.int32)
            s_copy.start()
            relay_copy(inner, my_slot).start()

        order = [None] + list(range(h - 1, -1, -1))
    else:
        order = list(range(h, levels)) + list(range(h - 1, -1, -1))

    b_copies = []
    near_copies = []
    for step in order:
        for i in range(INNER):
            if step == 0 and i == 0:
                continue
            target = far_mid if step is None else level_at(step)
            to = target * INNER + (inner + i) % INNER
            cp = pltpu.make_async_remote_copy(
                src_ref=blocks.at[to, 0],
                dst_ref=recv.at[me],
                send_sem=b_send.at[to],
                recv_sem=b_recv.at[me],
                device_id=(to, qi),
                device_id_type=MESH,
            )
            (b_copies if step is None or step >= h else near_copies).append(cp)

    def start(copies):
        for cp in copies:
            cp.start()

    if relay:

        @pl.when(is_mid)
        def _():
            start(b_copies + near_copies)
    else:
        start(b_copies + near_copies)

    strip = 128

    @pl.loop(0, nao // strip)
    def _(k):
        base = pl.multiple_of(k * strip, strip)
        nu = lax.broadcasted_iota(jnp.int32, (strip, nao), 0) + base
        perm[pl.ds(base, strip), :] = jnp.where(nu == batch[...][None, :], 1.0, 0.0).astype(jnp.bfloat16)

    def make_rows_t(r):
        rows_t[r] = lax.dot_general(
            c_all[r], perm[...], (((0,), (0,)), ((), ())), preferred_element_type=jnp.float32
        ).astype(jnp.bfloat16)

    for cp in c_own:
        cp.wait()

    @pl.loop(0, per)
    def _(j):
        make_rows_t(qi * per + j)

    if relay:

        @pl.when(is_end)
        def _():
            start(b_copies)

    def relay_transform(slab):
        x = rel_rows[...].reshape(half_rows, nao)
        rel_half[slab] = jnp.dot(
            x, c_all[slab], preferred_element_type=jnp.float32
        ).astype(jnp.bfloat16)

    early = (ni - 1) * per - 2

    def relay_early():
        a_local.wait()
        for step in range(h):
            for i in range(INNER):
                if step == 0 and i == 0:
                    continue
                at = ((lev % h + step) % h) * INNER + (inner + i) % INNER
                relay_copy(inner, at).wait_recv()

        @pl.loop(0, per)
        def _(j):
            relay_transform(qi * per + j)

    f_copies = []
    for d in range(1, ni):
        for j in range(per):
            t = (d - 1) * per + j
            slab = ((qi + ni - d) % ni) * per + j
            c_copies[t].wait_recv()
            cp = pltpu.make_async_remote_copy(
                src_ref=c_all.at[slab, part],
                dst_ref=c_all.at[slab, part],
                send_sem=f_send.at[t],
                recv_sem=f_recv.at[t],
                device_id=(sibling, qi),
                device_id_type=MESH,
            )
            cp.start()
            f_copies.append((cp, slab, t))
            if t >= 1:
                prev, prev_slab, _ = f_copies[t - 1]
                prev.wait_recv()
                make_rows_t(prev_slab)
            if relay and t == early:
                pl.when(is_mid)(relay_early)
    if relay:

        @pl.when(is_end)
        def _():
            start(near_copies)

    last, last_slab, _ = f_copies[-1]
    last.wait_recv()
    make_rows_t(last_slab)

    def p_copy(r):
        return pltpu.make_async_remote_copy(
            src_ref=p_out.at[r], dst_ref=p_in.at[r],
            send_sem=p_send.at[r], recv_sem=p_recv.at[r],
            device_id=(far_end * INNER + inner, qi), device_id_type=MESH,
        )

    if relay:

        @pl.when(is_mid)
        def _():
            s_copy.wait_recv()
            to_smem = pltpu.make_async_copy(sym_in, sym_s, s_own_sem)
            to_smem.start()
            to_smem.wait()

            @pl.loop(per, irr)
            def _(k):
                relay_transform((qi * per + k) % irr)

            their = sym_s[0, 0]

            @pl.loop(0, irr)
            def _(r):
                p_out[r] = jnp.dot(
                    rows_t[r, :, pl.ds(half_base, half_rows)],
                    rel_half[jnp.bitwise_xor(r, their)],
                    preferred_element_type=jnp.float32,
                ).astype(jnp.bfloat16)
                p_copy(r).start()

    own.wait()

    def do_level(step):
        lv = level_at(step)
        for i in range(INNER):
            if step == 0 and i == 0:
                continue
            src = lv * INNER + (inner + i) % INNER
            pltpu.make_async_remote_copy(
                src_ref=blocks.at[src, 0],
                dst_ref=recv.at[src],
                send_sem=b_send.at[src],
                recv_sem=b_recv.at[src],
                device_id=(src, qi),
                device_id_type=MESH,
            ).wait_recv()
        base = pl.multiple_of(lv * span, span)

        @pl.loop(0, irr)
        def _(c):
            x = recv[pl.ds(lv * INNER, INNER)].reshape(span, nao)
            half[c, pl.ds(base, span), :] = jnp.dot(
                x, c_all[c], preferred_element_type=jnp.float32
            ).astype(jnp.bfloat16)

    s = sym[0, 0]

    def masked(r, whole):
        a = lax.broadcasted_iota(jnp.int32, (VIR, VIR), 0)
        b = lax.broadcasted_iota(jnp.int32, (VIR, VIR), 1)
        live = (a < counts[r]) & (b < counts[jnp.bitwise_xor(r, s)])
        return jnp.where(live, whole, 0.0)

    def finish_all():
        @pl.loop(0, irr)
        def _(r):
            out[r] = masked(r, jnp.dot(
                rows_t[r], half[jnp.bitwise_xor(r, s)], preferred_element_type=jnp.float32
            ))

    if relay:
        other_base = pl.multiple_of((1 - hf) * half_rows, half_rows)

        def folded(r, base):
            return jnp.dot(
                rows_t[r, :, pl.ds(base, half_rows)],
                half[jnp.bitwise_xor(r, s), pl.ds(base, half_rows), :],
                preferred_element_type=jnp.float32,
            )

        do_level(0)

        @pl.when(is_mid)
        def _():
            for step in range(h, levels):
                do_level(step)

            @pl.loop(0, irr)
            def _(r):
                out[r] = folded(r, other_base)

        do_level(1)

        @pl.when(is_mid)
        def _():
            @pl.loop(0, irr)
            def _(r):
                out[r] = masked(r, out[r] + folded(r, half_base))

            for k in range(1, INNER):
                relay_copy((inner + k) % INNER, my_slot).wait_send()

            @pl.loop(0, irr)
            def _(r):
                p_copy(r).wait_send()

        @pl.when(is_end)
        def _():
            @pl.loop(0, irr)
            def _(r):
                out[r] = folded(r, half_base)

            @pl.loop(0, irr)
            def _(r):
                p_copy(r).wait_recv()
                out[r] = masked(r, out[r] + p_in[r].astype(jnp.float32))

            for k in range(INNER):
                relay_copy((inner + k) % INNER, my_slot).wait_send()
            s_copy.wait_send()
    else:
        for step in range(levels):
            do_level(step)
        finish_all()

    for cp in c_copies + b_copies + near_copies:
        cp.wait_send()
    for cp, _, _ in f_copies:
        cp.wait_send()


def body(n, ni, blocks, coefficients, shell_batch_functions, irrep_counts, pair_symmetry):
    rows, nao = blocks.shape[2], blocks.shape[3]
    per = coefficients.shape[1] // VIR
    irr = per * ni
    remote = max(1, (ni - 1) * per)
    dma = pltpu.SemaphoreType.DMA
    full = pl.pallas_call(
        functools.partial(kernel, n, ni),
        out_shape=jax.ShapeDtypeStruct((irr, VIR, VIR), jnp.float32),
        in_specs=[
            pl.BlockSpec(memory_space=pl.ANY),
            pl.BlockSpec(memory_space=pl.ANY),
            pl.BlockSpec(memory_space=pltpu.VMEM),
            pl.BlockSpec(memory_space=pltpu.SMEM),
            pl.BlockSpec(memory_space=pltpu.SMEM),
        ],
        out_specs=pl.BlockSpec(memory_space=pltpu.VMEM),
        scratch_shapes=[
            pltpu.VMEM((n, rows, nao), jnp.bfloat16),
            pltpu.VMEM((irr, nao, VIR), jnp.bfloat16),
            pltpu.VMEM((nao, nao), jnp.bfloat16),
            pltpu.VMEM((irr, VIR, nao), jnp.bfloat16),
            pltpu.VMEM((irr, nao, VIR), jnp.bfloat16),
            dma((n,)), dma((n,)), dma((remote,)), dma((remote,)),
            dma((remote,)), dma((remote,)), dma, dma((per,)),
            pltpu.VMEM((n // 2, rows, nao), jnp.bfloat16),
            pltpu.VMEM((irr, nao // 2, VIR), jnp.bfloat16),
            pltpu.VMEM((irr, VIR, VIR), jnp.bfloat16),
            pltpu.VMEM((irr, VIR, VIR), jnp.bfloat16),
            pltpu.VMEM((8, 128), jnp.int32),
            pltpu.VMEM((8, 128), jnp.int32),
            pltpu.SMEM((8, 128), jnp.int32),
            dma((INNER,)), dma((n // 2,)), dma((irr,)), dma((irr,)),
            dma, dma, dma, dma,
        ],
        compiler_params=pltpu.CompilerParams(
            collective_id=0, has_side_effects=True, vmem_limit_bytes=56 * 2**20
        ),
    )(blocks, coefficients, shell_batch_functions, pair_symmetry, irrep_counts)
    return full[None, None]


def solution(mesh):
    in_specs = (P(None, "irrep", "pair", None), P(None, "irrep"), P(), P(), P("pair", "irrep"))
    out_specs = P("pair", "irrep", None, None, None)
    return jax.shard_map(
        functools.partial(body, mesh.shape["pair"], mesh.shape["irrep"]),
        mesh=mesh, in_specs=in_specs, out_specs=out_specs, check_vma=False,
    )
```

```python
import functools

import jax
import jax.numpy as jnp
from jax import lax
from jax.experimental import pallas as pl
from jax.experimental.pallas import tpu as pltpu
from jax.sharding import PartitionSpec as P

VIR = 256
INNER = 4
MESH = pl.DeviceIdType.MESH


def kernel(
    n, ni, blocks, coef, batch, sym, counts, out,
    recv, c_all, perm, rows_t, half,
    b_send, b_recv, c_send, c_recv, f_send, f_recv, own_sem, c_own_sem,
    rel_rows, rel_half, p_out, p_in, sym_v, sym_in, sym_s,
    a_send, a_recv, p_send, p_recv, s_send, s_recv, a_own_sem, s_own_sem,
):
    me = lax.axis_index("pair")
    qi = lax.axis_index("irrep")
    rows = blocks.shape[2]
    nao = coef.shape[0]
    per = coef.shape[1] // VIR
    irr = ni * per
    levels = n // INNER
    h = levels // 2
    lev, inner, core = me // INNER, me % INNER, me % 2
    sibling = me + 1 - 2 * core
    span = INNER * rows
    relay = levels == 4
    hf = lev // h
    half_rows = h * span
    half_base = pl.multiple_of(hf * half_rows, half_rows)
    is_mid = ((lev + 1) // 2) % 2 == 1
    is_end = ((lev + 1) // 2) % 2 == 0
    own_mid, far_mid, far_end = 1 + hf, 2 - hf, 3 * (1 - hf)

    def level_at(step):
        if step < h:
            return (lev // h) * h + (lev % h + step) % h
        return ((lev // h + 1) % 2) * h + (lev % h + step) % h

    barrier = pltpu.get_barrier_semaphore()
    for k in range(1, n):
        pl.semaphore_signal(barrier, inc=1, device_id=((me + k) % n, qi), device_id_type=MESH)
    for d in range(1, ni):
        pl.semaphore_signal(barrier, inc=1, device_id=(me, (qi + d) % ni), device_id_type=MESH)
    own = pltpu.make_async_copy(blocks.at[me, 0], recv.at[me], own_sem)
    own.start()
    c_own = []
    for j in range(per):
        cp = pltpu.make_async_copy(
            coef.at[:, pl.ds(j * VIR, VIR)], c_all.at[qi * per + j], c_own_sem.at[j]
        )
        cp.start()
        c_own.append(cp)
    pl.semaphore_wait(barrier, n - 1 + ni - 1)

    part = pl.ds(pl.multiple_of(core * (nao // 2), nao // 2), nao // 2)
    other = pl.ds(pl.multiple_of((1 - core) * (nao // 2), nao // 2), nao // 2)
    c_copies = []
    for d in range(1, ni):
        for j in range(per):
            t = (d - 1) * per + j
            cp = pltpu.make_async_remote_copy(
                src_ref=coef.at[part, pl.ds(j * VIR, VIR)],
                dst_ref=c_all.at[qi * per + j, part],
                send_sem=c_send.at[t],
                recv_sem=c_recv.at[t],
                device_id=(me, (qi + d) % ni),
                device_id_type=MESH,
            )
            cp.start()
            c_copies.append(cp)

    def relay_copy(i, at):
        to = own_mid * INNER + i
        return pltpu.make_async_remote_copy(
            src_ref=blocks.at[far_end * INNER + i, 0],
            dst_ref=rel_rows.at[at],
            send_sem=a_send.at[i],
            recv_sem=a_recv.at[at],
            device_id=(to, qi),
            device_id_type=MESH,
        )

    my_slot = me - hf * h * INNER
    a_local = pltpu.make_async_copy(
        blocks.at[far_end * INNER + inner, 0], rel_rows.at[my_slot], a_own_sem
    )
    s_copy = pltpu.make_async_remote_copy(
        src_ref=sym_v, dst_ref=sym_in, send_sem=s_send, recv_sem=s_recv,
        device_id=(far_mid * INNER + inner, qi), device_id_type=MESH,
    )
    if relay:
        for k in range(1, INNER):
            relay_copy((inner + k) % INNER, my_slot).start()

        @pl.when(is_mid)
        def _():
            a_local.start()

        @pl.when(is_end)
        def _():
            sym_v[...] = jnp.full((8, 128), sym[0, 0], jnp.int32)
            s_copy.start()
            relay_copy(inner, my_slot).start()

        order = [None] + list(range(h - 1, -1, -1))
    else:
        order = list(range(h, levels)) + list(range(h - 1, -1, -1))

    b_copies = []
    near_copies = []
    for step in order:
        for i in range(INNER):
            if step == 0 and i == 0:
                continue
            target = far_mid if step is None else level_at(step)
            to = target * INNER + (inner + i) % INNER
            cp = pltpu.make_async_remote_copy(
                src_ref=blocks.at[to, 0],
                dst_ref=recv.at[me],
                send_sem=b_send.at[to],
                recv_sem=b_recv.at[me],
                device_id=(to, qi),
                device_id_type=MESH,
            )
            (b_copies if step is None or step >= h else near_copies).append(cp)

    def start(copies):
        for cp in copies:
            cp.start()

    if relay:

        @pl.when(is_mid)
        def _():
            start(b_copies + near_copies)
    else:
        start(b_copies + near_copies)

    strip = 128

    @pl.loop(0, nao // strip)
    def _(k):
        base = pl.multiple_of(k * strip, strip)
        nu = lax.broadcasted_iota(jnp.int32, (strip, nao), 0) + base
        perm[pl.ds(base, strip), :] = jnp.where(nu == batch[...][None, :], 1.0, 0.0).astype(jnp.bfloat16)

    def make_rows_t(r):
        rows_t[r] = lax.dot_general(
            c_all[r], perm[...], (((0,), (0,)), ((), ())), preferred_element_type=jnp.float32
        ).astype(jnp.bfloat16)

    for cp in c_own:
        cp.wait()

    @pl.loop(0, per)
    def _(j):
        make_rows_t(qi * per + j)

    if relay:

        @pl.when(is_end)
        def _():
            start(b_copies)

    def relay_transform(slab):
        x = rel_rows[...].reshape(half_rows, nao)
        rel_half[slab] = jnp.dot(
            x, c_all[slab], preferred_element_type=jnp.float32
        ).astype(jnp.bfloat16)

    early = (ni - 1) * per - 2

    def relay_early():
        a_local.wait()
        for step in range(h):
            for i in range(INNER):
                if step == 0 and i == 0:
                    continue
                at = ((lev % h + step) % h) * INNER + (inner + i) % INNER
                relay_copy(inner, at).wait_recv()

        @pl.loop(0, per)
        def _(j):
            relay_transform(qi * per + j)

    f_copies = []
    for d in range(1, ni):
        for j in range(per):
            t = (d - 1) * per + j
            slab = ((qi + ni - d) % ni) * per + j
            c_copies[t].wait_recv()
            cp = pltpu.make_async_remote_copy(
                src_ref=c_all.at[slab, part],
                dst_ref=c_all.at[slab, part],
                send_sem=f_send.at[t],
                recv_sem=f_recv.at[t],
                device_id=(sibling, qi),
                device_id_type=MESH,
            )
            cp.start()
            f_copies.append((cp, slab, t))
            if t >= 1:
                prev, prev_slab, _ = f_copies[t - 1]
                prev.wait_recv()
                make_rows_t(prev_slab)
            if relay and t == early:
                pl.when(is_mid)(relay_early)
            if relay and t == max(early - 1, 0):

                @pl.when(is_end)
                def _():
                    start(near_copies)

    last, last_slab, _ = f_copies[-1]
    last.wait_recv()
    make_rows_t(last_slab)

    def p_copy(r):
        return pltpu.make_async_remote_copy(
            src_ref=p_out.at[r], dst_ref=p_in.at[r],
            send_sem=p_send.at[r], recv_sem=p_recv.at[r],
            device_id=(far_end * INNER + inner, qi), device_id_type=MESH,
        )

    if relay:

        @pl.when(is_mid)
        def _():
            s_copy.wait_recv()
            to_smem = pltpu.make_async_copy(sym_in, sym_s, s_own_sem)
            to_smem.start()
            to_smem.wait()

            @pl.loop(per, irr)
            def _(k):
                relay_transform((qi * per + k) % irr)

            their = sym_s[0, 0]

            @pl.loop(0, irr)
            def _(r):
                p_out[r] = jnp.dot(
                    rows_t[r, :, pl.ds(half_base, half_rows)],
                    rel_half[jnp.bitwise_xor(r, their)],
                    preferred_element_type=jnp.float32,
                ).astype(jnp.bfloat16)
                p_copy(r).start()

    own.wait()

    def do_level(step):
        lv = level_at(step)
        for i in range(INNER):
            if step == 0 and i == 0:
                continue
            src = lv * INNER + (inner + i) % INNER
            pltpu.make_async_remote_copy(
                src_ref=blocks.at[src, 0],
                dst_ref=recv.at[src],
                send_sem=b_send.at[src],
                recv_sem=b_recv.at[src],
                device_id=(src, qi),
                device_id_type=MESH,
            ).wait_recv()
        base = pl.multiple_of(lv * span, span)

        @pl.loop(0, irr)
        def _(c):
            x = recv[pl.ds(lv * INNER, INNER)].reshape(span, nao)
            half[c, pl.ds(base, span), :] = jnp.dot(
                x, c_all[c], preferred_element_type=jnp.float32
            ).astype(jnp.bfloat16)

    s = sym[0, 0]

    def masked(r, whole):
        a = lax.broadcasted_iota(jnp.int32, (VIR, VIR), 0)
        b = lax.broadcasted_iota(jnp.int32, (VIR, VIR), 1)
        live = (a < counts[r]) & (b < counts[jnp.bitwise_xor(r, s)])
        return jnp.where(live, whole, 0.0)

    def finish_all():
        @pl.loop(0, irr)
        def _(r):
            out[r] = masked(r, jnp.dot(
                rows_t[r], half[jnp.bitwise_xor(r, s)], preferred_element_type=jnp.float32
            ))

    if relay:
        other_base = pl.multiple_of((1 - hf) * half_rows, half_rows)

        def folded(r, base):
            return jnp.dot(
                rows_t[r, :, pl.ds(base, half_rows)],
                half[jnp.bitwise_xor(r, s), pl.ds(base, half_rows), :],
                preferred_element_type=jnp.float32,
            )

        do_level(0)

        @pl.when(is_mid)
        def _():
            for step in range(h, levels):
                do_level(step)

            @pl.loop(0, irr)
            def _(r):
                out[r] = folded(r, other_base)

        do_level(1)

        @pl.when(is_mid)
        def _():
            @pl.loop(0, irr)
            def _(r):
                out[r] = masked(r, out[r] + folded(r, half_base))

            for k in range(1, INNER):
                relay_copy((inner + k) % INNER, my_slot).wait_send()

            @pl.loop(0, irr)
            def _(r):
                p_copy(r).wait_send()

        @pl.when(is_end)
        def _():
            @pl.loop(0, irr)
            def _(r):
                out[r] = folded(r, half_base)

            @pl.loop(0, irr)
            def _(r):
                p_copy(r).wait_recv()
                out[r] = masked(r, out[r] + p_in[r].astype(jnp.float32))

            for k in range(INNER):
                relay_copy((inner + k) % INNER, my_slot).wait_send()
            s_copy.wait_send()
    else:
        for step in range(levels):
            do_level(step)
        finish_all()

    for cp in c_copies + b_copies + near_copies:
        cp.wait_send()
    for cp, _, _ in f_copies:
        cp.wait_send()


def body(n, ni, blocks, coefficients, shell_batch_functions, irrep_counts, pair_symmetry):
    rows, nao = blocks.shape[2], blocks.shape[3]
    per = coefficients.shape[1] // VIR
    irr = per * ni
    remote = max(1, (ni - 1) * per)
    dma = pltpu.SemaphoreType.DMA
    full = pl.pallas_call(
        functools.partial(kernel, n, ni),
        out_shape=jax.ShapeDtypeStruct((irr, VIR, VIR), jnp.float32),
        in_specs=[
            pl.BlockSpec(memory_space=pl.ANY),
            pl.BlockSpec(memory_space=pl.ANY),
            pl.BlockSpec(memory_space=pltpu.VMEM),
            pl.BlockSpec(memory_space=pltpu.SMEM),
            pl.BlockSpec(memory_space=pltpu.SMEM),
        ],
        out_specs=pl.BlockSpec(memory_space=pltpu.VMEM),
        scratch_shapes=[
            pltpu.VMEM((n, rows, nao), jnp.bfloat16),
            pltpu.VMEM((irr, nao, VIR), jnp.bfloat16),
            pltpu.VMEM((nao, nao), jnp.bfloat16),
            pltpu.VMEM((irr, VIR, nao), jnp.bfloat16),
            pltpu.VMEM((irr, nao, VIR), jnp.bfloat16),
            dma((n,)), dma((n,)), dma((remote,)), dma((remote,)),
            dma((remote,)), dma((remote,)), dma, dma((per,)),
            pltpu.VMEM((n // 2, rows, nao), jnp.bfloat16),
            pltpu.VMEM((irr, nao // 2, VIR), jnp.bfloat16),
            pltpu.VMEM((irr, VIR, VIR), jnp.bfloat16),
            pltpu.VMEM((irr, VIR, VIR), jnp.bfloat16),
            pltpu.VMEM((8, 128), jnp.int32),
            pltpu.VMEM((8, 128), jnp.int32),
            pltpu.SMEM((8, 128), jnp.int32),
            dma((INNER,)), dma((n // 2,)), dma((irr,)), dma((irr,)),
            dma, dma, dma, dma,
        ],
        compiler_params=pltpu.CompilerParams(
            collective_id=0, has_side_effects=True, vmem_limit_bytes=56 * 2**20
        ),
    )(blocks, coefficients, shell_batch_functions, pair_symmetry, irrep_counts)
    return full[None, None]


def solution(mesh):
    in_specs = (P(None, "irrep", "pair", None), P(None, "irrep"), P(), P(), P("pair", "irrep"))
    out_specs = P("pair", "irrep", None, None, None)
    return jax.shard_map(
        functools.partial(body, mesh.shape["pair"], mesh.shape["irrep"]),
        mesh=mesh, in_specs=in_specs, out_specs=out_specs, check_vma=False,
    )
```
